32 devices in a mesh: blk: 8 (over y, x, core), uly: 4 (over z).
Axes of the slice: x: 2, y: 2, z: 4, core: 2. Of those that a mesh axis runs over, the one named last changes fastest.
Arguments:
- tokens: bfloat16 [1536, 2048], P(('blk', 'uly')), may hold values from -6 to 6
- mod_shift: float32 [2048], replicated, may hold values from -3 to 3
- mod_scale: float32 [2048], replicated, may hold values from -2.5 to 2.5
- mod_gate: float32 [2048], replicated, may hold values from 0.25 to 1.5
- w_query: bfloat16 [2048, 2048], P(None, 'uly'), may hold values from -0.125 to 0.125
- w_key: bfloat16 [2048, 2048], P(None, 'uly'), may hold values from -0.125 to 0.125
- w_value: bfloat16 [2048, 2048], P(None, 'uly'), may hold values from -0.125 to 0.125
- w_out: bfloat16 [2048, 2048], P('uly'), may hold values from -0.125 to 0.125
- score_gain: float32 [32], replicated, may hold values from 4 to 40, as said below
Outputs:
- block_out: bfloat16 [1536, 2048], P(('blk', 'uly'))
The draws below stay inside these ranges and needn't reach their ends.
Inputs may be any that keep to these rules, and one draw needn't show every extreme that they name: `score_gain`: one positive factor for each head.
All inputs are finite; a program needn't handle non-finite values.
Results may differ from the reference program's by a relative error of at most 0.012.
The reference program's roundings to bfloat16 on the way (of `modded`, `value`, `weights` and `attended`) count: a program that leaves them out, or rounds other values in their place, can miss the bound.
Values may be sent and summed in bfloat16 or wider, within the bound.
A program may use at most 192 MiB of HBM per device.

```python
import math
import jax
import jax.numpy as jnp
from jax import lax

D = 2048
HEADS = 32
SEQ = 1536


def draw_score_gain(key, part):
    level = jax.random.uniform(key, (HEADS,), jnp.float32)
    return 4.0 * jnp.exp(level * jnp.log(4.0))


def block_scale(stream_key, dims, shards, smallest, largest):
    factor_of, own = 1.0, jax.random.fold_in(stream_key, 6)
    for position, blocks in shards:
        draws = jnp.exp(jax.random.uniform(jax.random.fold_in(own, position), (blocks,), jnp.float32, smallest / len(shards), largest / len(shards)))
        factor_of = factor_of * jnp.repeat(draws, dims[position] // blocks).reshape([-1 if axis == position else 1 for axis in range(len(dims))])
    return factor_of


def centred(rng, extent, scale, limit, cuts=(), held_as=jnp.bfloat16):
    level = block_scale(rng, extent, cuts, -0.22, 0.18) if cuts else 1.0
    entries = jax.random.normal(rng, extent, jnp.float32) * scale * level
    return jnp.minimum(jnp.maximum(entries, -limit), limit).astype(held_as)


def setup_inputs(seed: int = 0) -> dict:
    arg_keys = jax.random.split(jax.random.key(seed), 10)
    tokens = centred(arg_keys[0], (SEQ, D), 1.0, 6.0, ((0, 32),))
    mod_shift = centred(arg_keys[1], (D,), 0.5, 3.0, (), jnp.float32)
    mod_scale = centred(arg_keys[2], (D,), 0.5, 2.5, (), jnp.float32)
    mod_gate = jnp.clip(jax.random.uniform(arg_keys[3], (D,), jnp.float32, 0.25, 1.5), 0.25, 1.5)
    w_query = centred(arg_keys[4], (D, D), D ** -0.5, 0.125, ((1, 4),))
    w_key = centred(arg_keys[5], (D, D), D ** -0.5, 0.125, ((1, 4),))
    w_value = centred(arg_keys[6], (D, D), D ** -0.5, 0.125, ((1, 4),))
    w_out = centred(arg_keys[7], (D, D), D ** -0.5, 0.125, ((0, 4),))
    score_gain = draw_score_gain(jax.random.fold_in(arg_keys[9], 71), 0)
    return {"tokens": tokens, "mod_shift": mod_shift, "mod_scale": mod_scale, "mod_gate": mod_gate, "w_query": w_query, "w_key": w_key, "w_value": w_value, "w_out": w_out, "score_gain": score_gain}


def modulate(tokens, mod_shift, mod_scale):
    values = tokens.astype(jnp.float32)
    center = values - lax.optimization_barrier(jnp.mean(values, axis=-1, keepdims=True))
    spread = lax.optimization_barrier(jnp.mean(center * center, axis=-1, keepdims=True))
    normed = center * lax.rsqrt(spread + 1e-06)
    return (normed * (1.0 + mod_scale) + mod_shift).astype(jnp.bfloat16)

def head_norm(projected, width):
    count = projected.shape[0]
    split = projected.reshape(count, -1, width)
    power = lax.optimization_barrier(jnp.mean(split * split, axis=-1, keepdims=True))
    return (split * lax.rsqrt(power + 1e-06)).reshape(count, -1).astype(jnp.bfloat16)

def reference(tokens, mod_shift, mod_scale, mod_gate, w_query, w_key, w_value, w_out, score_gain):
    width = D // HEADS
    modded = modulate(tokens, mod_shift, mod_scale)
    query = head_norm(jnp.dot(modded, w_query, preferred_element_type=jnp.float32), width)
    key = head_norm(jnp.dot(modded, w_key, preferred_element_type=jnp.float32), width)
    value = jnp.dot(modded, w_value, preferred_element_type=jnp.float32).astype(jnp.bfloat16)
    query_heads = query.reshape(SEQ, HEADS, width).transpose(1, 0, 2)
    key_heads = key.reshape(SEQ, HEADS, width).transpose(1, 0, 2)
    value_heads = value.reshape(SEQ, HEADS, width).transpose(1, 0, 2)
    block_rows = math.gcd(SEQ, 1024)

    def one_head(packed):
        query_head, key_head, value_head, gain = packed
        factor = gain / math.sqrt(width)

        def one_block(query_block):
            scores = jnp.dot(query_block, key_head.T, preferred_element_type=jnp.float32) * factor
            top = lax.optimization_barrier(jnp.max(scores, axis=-1, keepdims=True))
            expo = jnp.exp(scores - top)
            total = lax.optimization_barrier(jnp.sum(expo, axis=-1, keepdims=True))
            weights = expo.astype(jnp.bfloat16)
            summed = jnp.dot(weights, value_head, preferred_element_type=jnp.float32)
            return (summed / total).astype(jnp.bfloat16)
        blocks = query_head.reshape(SEQ // block_rows, block_rows, width)
        return lax.map(one_block, blocks).reshape(SEQ, width)
    attended = lax.map(one_head, (query_heads, key_heads, value_heads, score_gain))
    attended = attended.transpose(1, 0, 2).reshape(SEQ, D)
    projected = jnp.dot(attended, w_out, preferred_element_type=jnp.float32)
    return (tokens.astype(jnp.float32) + mod_gate * projected).astype(jnp.bfloat16)
```

```python
import functools
import math

import jax
import jax.numpy as jnp
from jax import lax
from jax.experimental import pallas as pl
from jax.experimental.pallas import tpu as pltpu
from jax.sharding import PartitionSpec as P

D = 2048
HEADS = 32
LOG2E = math.log2(math.e)
MESH = pl.DeviceIdType.MESH


def kernel(
    nb, nz, tok, shift, scale, gate, gain, wq, wk, wv, wo, out,
    mod, wq_v, wk_v, wv_v, wo_v, snd, rcv, asnd, arcv, own, rsnd, rrcv,
    wsem, gs, gr, hs, hr, bs, br, rs, rr,
):
    width = D // HEADS
    rows = tok.shape[0]
    block = nz * rows
    half = block // 2
    tile = rrcv.shape[-1]
    parts = D // tile
    mb, mz = lax.axis_index("blk"), lax.axis_index("uly")

    loads = [
        pltpu.make_async_copy(src, dst, wsem.at[i])
        for i, (src, dst) in enumerate(((wq, wq_v), (wk, wk_v), (wv, wv_v), (wo, wo_v)))
    ]
    for load in loads:
        load.start()

    barrier = pltpu.get_barrier_semaphore()
    for j in range(1, nz):
        pl.semaphore_signal(barrier, inc=1, device_id={"uly": lax.rem(mz + j, nz)}, device_id_type=MESH)
    for j in range(1, nb):
        pl.semaphore_signal(barrier, inc=1, device_id={"blk": lax.rem(mb + j, nb)}, device_id_type=MESH)

    def order(k):
        if nz != 4:
            return lax.rem(mz + k, nz)
        high = mz // 2
        near = mz + 1 - 2 * lax.rem(mz, 2)
        return jnp.where(k == 0, mz, jnp.where(k == 1, near, jnp.where(k == 2, 2 - high, 3 - 3 * high)))

    values = tok[...].astype(jnp.float32)
    center = values - jnp.mean(values, axis=-1, keepdims=True)
    spread = jnp.mean(center * center, axis=-1, keepdims=True)
    normed = center * lax.rsqrt(spread + 1e-06)
    mod[mz] = (normed * (1.0 + scale[...]) + shift[...]).astype(jnp.bfloat16)

    pl.semaphore_wait(barrier, nz - 1 + nb - 1)

    def gather(z):
        return pltpu.make_async_remote_copy(
            src_ref=mod.at[mz], dst_ref=mod.at[mz], send_sem=gs.at[z], recv_sem=gr.at[mz],
            device_id={"uly": z}, device_id_type=MESH)

    def gathered(z):
        return pltpu.make_async_remote_copy(
            src_ref=mod.at[z], dst_ref=mod.at[z], send_sem=gs.at[z], recv_sem=gr.at[z],
            device_id={"uly": z}, device_id_type=MESH)

    for k in range(nz - 1, 0, -1):
        gather(order(k)).start()
    for load in loads[:3]:
        load.wait()

    def spot(b, z):
        return pl.ds(pl.multiple_of((b * nz + z) * rows, rows), rows)

    def heads_to(z, b):
        return pltpu.make_async_remote_copy(
            src_ref=snd.at[z, b], dst_ref=rcv.at[:, spot(mb, z), :], send_sem=hs.at[z, b],
            recv_sem=hr.at[z, mb], device_id={"blk": b}, device_id_type=MESH)

    def heads_from(z, b):
        return pltpu.make_async_remote_copy(
            src_ref=snd.at[z, b], dst_ref=rcv.at[:, spot(b, z), :], send_sem=hs.at[z, b],
            recv_sem=hr.at[z, b], device_id={"blk": b}, device_id_type=MESH)

    def piece(k, carry):
        z = order(k)

        @pl.when(k > 0)
        def _():
            gathered(z).wait_recv()

        x = mod[z]
        query = jnp.dot(x, wq_v[...], preferred_element_type=jnp.float32)
        key = jnp.dot(x, wk_v[...], preferred_element_type=jnp.float32)
        value = jnp.dot(x, wv_v[...], preferred_element_type=jnp.float32)

        def unit(part):
            power = jnp.mean(part * part, axis=-1, keepdims=True)
            return part * lax.rsqrt(power + 1e-06)

        for h in range(nb):
            cols = slice(h * width, (h + 1) * width)
            snd[z, h, 0] = jnp.concatenate([unit(key[:, cols]), value[:, cols]], axis=1).astype(jnp.bfloat16)
            line = unit(query[:, cols])
            snd[z, h, 1] = jnp.concatenate([line, jnp.zeros_like(line)], axis=1).astype(jnp.bfloat16)
        rcv[:, spot(mb, z), :] = snd[z, mb]

        def send(j, carry):
            heads_to(z, lax.rem(mb + j, nb)).start()
            return carry

        lax.fori_loop(1, nb, send, 0)
        return carry

    lax.fori_loop(0, nz, piece, 0)

    def arrive(i, carry):
        heads_from(order(i // (nb - 1)), lax.rem(mb + 1 + lax.rem(i, nb - 1), nb)).wait_recv()
        return carry

    lax.fori_loop(0, nz * (nb - 1), arrive, 0)

    factor = gain[mz * nb + mb] * (LOG2E / math.sqrt(width))

    def back_to(b):
        return pltpu.make_async_remote_copy(
            src_ref=asnd.at[b], dst_ref=arcv.at[mb], send_sem=bs.at[b], recv_sem=br.at[mb],
            device_id={"blk": b}, device_id_type=MESH)

    def back_from(b):
        return pltpu.make_async_remote_copy(
            src_ref=asnd.at[b], dst_ref=arcv.at[b], send_sem=bs.at[b], recv_sem=br.at[b],
            device_id={"blk": b}, device_id_type=MESH)

    def attend(k, carry):
        b = lax.rem(mb + k, nb)
        q = rcv[1, pl.ds(pl.multiple_of(b * block, block), block), :]
        kv = rcv[0]
        scores = lax.dot_general(q, kv, (((1,), (1,)), ((), ())), preferred_element_type=jnp.float32)
        top = jnp.max(scores, axis=-1, keepdims=True)
        expo = jnp.exp2((scores - top) * factor)
        total = jnp.sum(expo, axis=-1, keepdims=True)
        summed = jnp.dot(expo.astype(jnp.bfloat16), kv, preferred_element_type=jnp.float32) / total
        packed = jnp.concatenate([summed[:half, width:], summed[half:, width:]], axis=1)
        asnd[b] = packed.astype(jnp.bfloat16)

        @pl.when(k < nb)
        def _():
            back_to(b).start()

        return carry

    lax.fori_loop(1, nb + 1, attend, 0)
    arcv[mb] = asnd[mb]
    loads[3].wait()
    for j in range(1, nb):
        back_from(lax.rem(mb + j, nb)).wait_recv()

    pieces = [arcv[h] for h in range(nb)]
    attended = jnp.concatenate(
        [
            jnp.concatenate([part[:, :width] for part in pieces], axis=1),
            jnp.concatenate([part[:, width:] for part in pieces], axis=1),
        ],
        axis=0,
    )

    def sum_to(n, z):
        return pltpu.make_async_remote_copy(
            src_ref=rsnd.at[n, z], dst_ref=rrcv.at[n, mz], send_sem=rs.at[n, z], recv_sem=rr.at[n, mz],
            device_id={"uly": z}, device_id_type=MESH)

    def sum_from(n, z):
        return pltpu.make_async_remote_copy(
            src_ref=rsnd.at[n, z], dst_ref=rrcv.at[n, z], send_sem=rs.at[n, z], recv_sem=rr.at[n, z],
            device_id={"uly": z}, device_id_type=MESH)

    for n in range(parts):
        part = jnp.dot(attended, wo_v[:, n * tile : (n + 1) * tile], preferred_element_type=jnp.float32)
        for z in range(nz):
            own[n, z] = part[z * rows : (z + 1) * rows]
            rsnd[n, z] = part[z * rows : (z + 1) * rows].astype(jnp.bfloat16)
        for k in range(nz - 1, 0, -1):
            sum_to(n, order(k)).start()
    for n in range(parts):
        total = own[n, mz]
        for k in range(1, nz):
            z = order(k)
            sum_from(n, z).wait_recv()
            total = total + rrcv[n, z].astype(jnp.float32)
        cols = slice(n * tile, (n + 1) * tile)
        out[:, cols] = (tok[:, cols].astype(jnp.float32) + gate[:, cols] * total).astype(jnp.bfloat16)

    for k in range(1, nz):
        gather(order(k)).wait_send()

    def sent(i, carry):
        heads_to(order(i // (nb - 1)), lax.rem(mb + 1 + lax.rem(i, nb - 1), nb)).wait_send()
        return carry

    lax.fori_loop(0, nz * (nb - 1), sent, 0)
    for j in range(1, nb):
        back_to(lax.rem(mb + j, nb)).wait_send()
    for n in range(parts):
        for k in range(1, nz):
            sum_to(n, order(k)).wait_send()


def fused(nb, nz, tokens, mod_shift, mod_scale, mod_gate, w_query, w_key, w_value, w_out, score_gain):
    rows = tokens.shape[0]
    cols = w_query.shape[1]
    tile = 512
    parts = D // tile
    bf16, f32 = jnp.bfloat16, jnp.float32
    vmem = pl.BlockSpec(memory_space=pltpu.VMEM)
    smem = pl.BlockSpec(memory_space=pltpu.SMEM)
    anywhere = pl.BlockSpec(memory_space=pl.ANY)
    dma = pltpu.SemaphoreType.DMA
    return pl.pallas_call(
        functools.partial(kernel, nb, nz),
        out_shape=jax.ShapeDtypeStruct((rows, D), bf16),
        in_specs=[vmem] * 4 + [smem] + [anywhere] * 4,
        out_specs=vmem,
        scratch_shapes=[
            pltpu.VMEM((nz, rows, D), bf16),
            pltpu.VMEM((D, cols), bf16),
            pltpu.VMEM((D, cols), bf16),
            pltpu.VMEM((D, cols), bf16),
            pltpu.VMEM((cols, D), bf16),
            pltpu.VMEM((nz, nb, 2, rows, 128), bf16),
            pltpu.VMEM((2, nb * nz * rows, 128), bf16),
            pltpu.VMEM((nb, nz * rows // 2, 128), bf16),
            pltpu.VMEM((nb, nz * rows // 2, 128), bf16),
            pltpu.VMEM((parts, nz, rows, tile), f32),
            pltpu.VMEM((parts, nz, rows, tile), bf16),
            pltpu.VMEM((parts, nz, rows, tile), bf16),
            dma((4,)),
            dma((nz,)),
            dma((nz,)),
            dma((nz, nb)),
            dma((nz, nb)),
            dma((nb,)),
            dma((nb,)),
            dma((parts, nz)),
            dma((parts, nz)),
        ],
        compiler_params=pltpu.CompilerParams(
            collective_id=0, has_side_effects=True, vmem_limit_bytes=40 * 1024 * 1024
        ),
    )(
        tokens, mod_shift[None], mod_scale[None], mod_gate[None], score_gain,
        w_query, w_key, w_value, w_out,
    )


def modulate(tokens, mod_shift, mod_scale):
    values = tokens.astype(jnp.float32)
    center = values - jnp.mean(values, axis=-1, keepdims=True)
    spread = jnp.mean(center * center, axis=-1, keepdims=True)
    normed = center * lax.rsqrt(spread + 1e-06)
    return (normed * (1.0 + mod_scale) + mod_shift).astype(jnp.bfloat16)


def head_norm(projected, width):
    count = projected.shape[0]
    split = projected.reshape(count, -1, width)
    power = jnp.mean(split * split, axis=-1, keepdims=True)
    return (split * lax.rsqrt(power + 1e-06)).reshape(count, -1).astype(jnp.bfloat16)


def body(tokens, mod_shift, mod_scale, mod_gate, w_query, w_key, w_value, w_out, score_gain):
    width = D // HEADS
    local_cols = w_query.shape[1]
    local_heads = local_cols // width
    modded = modulate(tokens, mod_shift, mod_scale)
    piece = lax.all_gather(modded, "uly", axis=0, tiled=True)
    joined = jnp.concatenate(
        [
            jnp.dot(piece, w_query, preferred_element_type=jnp.float32),
            jnp.dot(piece, w_key, preferred_element_type=jnp.float32),
            jnp.dot(piece, w_value, preferred_element_type=jnp.float32),
        ],
        axis=1,
    )
    queries = head_norm(joined[:, :local_cols], width)
    keys = head_norm(joined[:, local_cols : 2 * local_cols], width)
    values = joined[:, 2 * local_cols :].astype(jnp.bfloat16)
    gains = lax.dynamic_slice_in_dim(score_gain, lax.axis_index("uly") * local_heads, local_heads)
    factors = gains / math.sqrt(width)
    rows = queries.shape[0]
    query_heads = queries.reshape(rows, local_heads, width)
    initial = (
        jnp.full((local_heads, rows), -jnp.inf, jnp.float32),
        jnp.zeros((local_heads, rows), jnp.float32),
        jnp.zeros((local_heads, rows, width), jnp.float32),
    )
    key_piece = lax.all_gather(keys, "blk", axis=0, tiled=True)
    value_piece = lax.all_gather(values, "blk", axis=0, tiled=True)
    count = key_piece.shape[0]
    groups = count // rows
    limit = max(rows, 1024)
    depth = max(
        [step for step in range(1, groups + 1) if groups % step == 0 and step * rows <= limit]
    )
    stride = depth * rows
    key_blocks = key_piece.reshape(count // stride, stride, local_heads, width)
    value_blocks = value_piece.reshape(count // stride, stride, local_heads, width)

    def one_block(carry, blocks):
        run_max, run_total, run_acc = carry
        key_block, value_block = blocks
        scores = jnp.einsum(
            "rhd,khd->hrk", query_heads, key_block, preferred_element_type=jnp.float32
        )
        scores = scores * factors[:, None, None]
        new_max = jnp.maximum(run_max, jnp.max(scores, axis=-1))
        expo = jnp.exp(scores - new_max[..., None])
        rescale = jnp.exp(run_max - new_max)
        new_total = run_total * rescale + jnp.sum(expo, axis=-1)
        summed = jnp.einsum(
            "hrk,khd->hrd",
            expo.astype(jnp.bfloat16),
            value_block,
            preferred_element_type=jnp.float32,
        )
        new_acc = run_acc * rescale[..., None] + summed
        return ((new_max, new_total, new_acc), None)

    result, unused = lax.scan(one_block, initial, (key_blocks, value_blocks))
    run_max, run_total, run_acc = result
    attended = (run_acc / run_total[..., None]).astype(jnp.bfloat16)
    attended = attended.transpose(1, 0, 2).reshape(rows, local_cols)
    returned = lax.all_to_all(attended, "uly", split_axis=0, concat_axis=1, tiled=True)
    projected = jnp.dot(
        returned,
        lax.all_gather(w_out, "uly", axis=0, tiled=True),
        preferred_element_type=jnp.float32,
    )
    return (tokens.astype(jnp.float32) + mod_gate * projected).astype(jnp.bfloat16)


def solution(mesh):
    in_specs = (
        P(("blk", "uly"), None),
        P(),
        P(),
        P(),
        P(None, "uly"),
        P(None, "uly"),
        P(None, "uly"),
        P("uly", None),
        P(),
    )
    out_specs = P(("blk", "uly"), None)
    nb, nz = mesh.shape["blk"], mesh.shape["uly"]
    run = body
    if HEADS == nb * nz:
        run = functools.partial(fused, nb, nz)
    return jax.shard_map(run, mesh=mesh, in_specs=in_specs, out_specs=out_specs, check_vma=False)
```

```python
import functools
import math

import jax
import jax.numpy as jnp
from jax import lax
from jax.experimental import pallas as pl
from jax.experimental.pallas import tpu as pltpu
from jax.sharding import PartitionSpec as P

D = 2048
HEADS = 32
LOG2E = math.log2(math.e)
MESH = pl.DeviceIdType.MESH


def kernel(
    nb, nz, tok_h, shift_h, scale_h, gate_h, gain_h, wq, wk, wv, wo, out,
    tok, shift, scale, gate, gain, mod, wq_v, wk_v, wv_v, wo_v, snd, rcv, asnd, arcv, own, rsnd, rrcv,
    wsem, gs, gr, fs, hs, hr, bs, br, rs, rr,
):
    width = D // HEADS
    rows = tok.shape[0]
    block = nz * rows
    half = block // 2
    tile = rrcv.shape[-1]
    parts = D // tile
    mb, mz = lax.axis_index("blk"), lax.axis_index("uly")

    pairs = (
        (tok_h, tok), (shift_h, shift), (scale_h, scale), (wq, wq_v), (wk, wk_v), (wv, wv_v),
        (wo, wo_v), (gate_h, gate), (gain_h, gain),
    )
    loads = [
        pltpu.make_async_copy(src, dst, wsem.at[i])
        for i, (src, dst) in enumerate(pairs)
    ]
    for load in loads:
        load.start()

    barrier = pltpu.get_barrier_semaphore()
    for j in range(1, nz):
        pl.semaphore_signal(barrier, inc=1, device_id={"uly": lax.rem(mz + j, nz)}, device_id_type=MESH)
    for j in range(1, nb):
        pl.semaphore_signal(barrier, inc=1, device_id={"blk": lax.rem(mb + j, nb)}, device_id_type=MESH)

    def order(k):
        if nz != 4:
            return lax.rem(mz + k, nz)
        high = mz // 2
        near = mz + 1 - 2 * lax.rem(mz, 2)
        return jnp.where(k == 0, mz, jnp.where(k == 1, near, jnp.where(k == 2, 2 - high, 3 - 3 * high)))

    for load in loads[:3]:
        load.wait()
    relayed = nz == 4
    direct = (2, 1) if relayed else tuple(range(nz - 1, 0, -1))
    middle = (mz + 1) // 2 == 1

    values = tok[...].astype(jnp.float32)
    center = values - jnp.mean(values, axis=-1, keepdims=True)
    spread = jnp.mean(center * center, axis=-1, keepdims=True)
    normed = center * lax.rsqrt(spread + 1e-06)
    mod[mz] = (normed * (1.0 + scale[...]) + shift[...]).astype(jnp.bfloat16)

    pl.semaphore_wait(barrier, nz - 1 + nb - 1)

    def gather(z):
        return pltpu.make_async_remote_copy(
            src_ref=mod.at[mz], dst_ref=mod.at[mz], send_sem=gs.at[z], recv_sem=gr.at[mz],
            device_id={"uly": z}, device_id_type=MESH)

    def gathered(z):
        return pltpu.make_async_remote_copy(
            src_ref=mod.at[z], dst_ref=mod.at[z], send_sem=gs.at[z], recv_sem=gr.at[z],
            device_id={"uly": z}, device_id_type=MESH)

    def forward(z):
        return pltpu.make_async_remote_copy(
            src_ref=mod.at[z], dst_ref=mod.at[z], send_sem=fs.at[z], recv_sem=gr.at[z],
            device_id={"uly": order(1)}, device_id_type=MESH)

    for k in direct:
        gather(order(k)).start()
    for load in loads[3:6]:
        load.wait()

    def spot(b, z):
        return pl.ds(pl.multiple_of((b * nz + z) * rows, rows), rows)

    def heads_to(z, b):
        return pltpu.make_async_remote_copy(
            src_ref=snd.at[z, b], dst_ref=rcv.at[:, spot(mb, z), :], send_sem=hs.at[z, b],
            recv_sem=hr.at[z, mb], device_id={"blk": b}, device_id_type=MESH)

    def heads_from(z, b):
        return pltpu.make_async_remote_copy(
            src_ref=snd.at[z, b], dst_ref=rcv.at[:, spot(b, z), :], send_sem=hs.at[z, b],
            recv_sem=hr.at[z, b], device_id={"blk": b}, device_id_type=MESH)

    def piece(k, carry):
        z = order(k)

        @pl.when(k > 0)
        def _():
            gathered(z).wait_recv()

        if relayed:

            @pl.when((k > 1) & middle)
            def _():
                forward(z).start()

        x = mod[z]
        query = jnp.dot(x, wq_v[...], preferred_element_type=jnp.float32)
        key = jnp.dot(x, wk_v[...], preferred_element_type=jnp.float32)
        value = jnp.dot(x, wv_v[...], preferred_element_type=jnp.float32)

        def unit(part):
            power = jnp.mean(part * part, axis=-1, keepdims=True)
            return part * lax.rsqrt(power + 1e-06)

        for h in range(nb):
            cols = slice(h * width, (h + 1) * width)
            snd[z, h, 0] = jnp.concatenate([unit(key[:, cols]), value[:, cols]], axis=1).astype(jnp.bfloat16)
            line = unit(query[:, cols])
            snd[z, h, 1] = jnp.concatenate([line, jnp.zeros_like(line)], axis=1).astype(jnp.bfloat16)
        rcv[:, spot(mb, z), :] = snd[z, mb]

        def send(j, carry):
            heads_to(z, lax.rem(mb + j, nb)).start()
            return carry

        lax.fori_loop(1, nb, send, 0)
        return carry

    lax.fori_loop(0, nz, piece, 0)

    def arrive(i, carry):
        heads_from(order(i // (nb - 1)), lax.rem(mb + 1 + lax.rem(i, nb - 1), nb)).wait_recv()
        return carry

    lax.fori_loop(0, nz * (nb - 1), arrive, 0)

    loads[8].wait()
    chosen = lax.broadcasted_iota(jnp.int32, gain.shape, 1) == mz * nb + mb
    factor = jnp.sum(jnp.where(chosen, gain[...], 0.0), axis=-1, keepdims=True) * (LOG2E / math.sqrt(width))

    def back_to(b):
        return pltpu.make_async_remote_copy(
            src_ref=asnd.at[b], dst_ref=arcv.at[mb], send_sem=bs.at[b], recv_sem=br.at[mb],
            device_id={"blk": b}, device_id_type=MESH)

    def back_from(b):
        return pltpu.make_async_remote_copy(
            src_ref=asnd.at[b], dst_ref=arcv.at[b], send_sem=bs.at[b], recv_sem=br.at[b],
            device_id={"blk": b}, device_id_type=MESH)

    def attend(k, carry):
        b = lax.rem(mb + k, nb)
        q = rcv[1, pl.ds(pl.multiple_of(b * block, block), block), :]
        kv = rcv[0]
        scores = lax.dot_general(q, kv, (((1,), (1,)), ((), ())), preferred_element_type=jnp.float32)
        top = jnp.max(scores, axis=-1, keepdims=True)
        expo = jnp.exp2((scores - top) * factor)
        total = jnp.sum(expo, axis=-1, keepdims=True)
        summed = jnp.dot(expo.astype(jnp.bfloat16), kv, preferred_element_type=jnp.float32) / total
        packed = jnp.concatenate([summed[:half, width:], summed[half:, width:]], axis=1)
        asnd[b] = packed.astype(jnp.bfloat16)

        @pl.when(k < nb)
        def _():
            back_to(b).start()

        return carry

    lax.fori_loop(1, nb + 1, attend, 0)
    arcv[mb] = asnd[mb]
    loads[6].wait()
    loads[7].wait()
    for j in range(1, nb):
        back_from(lax.rem(mb + j, nb)).wait_recv()

    pieces = [arcv[h] for h in range(nb)]
    attended = jnp.concatenate(
        [
            jnp.concatenate([part[:, :width] for part in pieces], axis=1),
            jnp.concatenate([part[:, width:] for part in pieces], axis=1),
        ],
        axis=0,
    )

    def sum_to(n, z):
        return pltpu.make_async_remote_copy(
            src_ref=rsnd.at[n, z], dst_ref=rrcv.at[n, mz], send_sem=rs.at[n, z], recv_sem=rr.at[n, mz],
            device_id={"uly": z}, device_id_type=MESH)

    def sum_from(n, z):
        return pltpu.make_async_remote_copy(
            src_ref=rsnd.at[n, z], dst_ref=rrcv.at[n, z], send_sem=rs.at[n, z], recv_sem=rr.at[n, z],
            device_id={"uly": z}, device_id_type=MESH)

    for n in range(parts):
        part = jnp.dot(attended, wo_v[:, n * tile : (n + 1) * tile], preferred_element_type=jnp.float32)
        for z in range(nz):
            own[n, z] = part[z * rows : (z + 1) * rows]
            rsnd[n, z] = part[z * rows : (z + 1) * rows].astype(jnp.bfloat16)
        for k in range(nz - 1, 0, -1):
            sum_to(n, order(k)).start()
    for n in range(parts):
        total = own[n, mz]
        for k in range(1, nz):
            z = order(k)
            sum_from(n, z).wait_recv()
            total = total + rrcv[n, z].astype(jnp.float32)
        cols = slice(n * tile, (n + 1) * tile)
        out[:, cols] = (tok[:, cols].astype(jnp.float32) + gate[:, cols] * total).astype(jnp.bfloat16)

    for k in direct:
        gather(order(k)).wait_send()
    if relayed:

        @pl.when(middle)
        def _():
            for k in (2, 3):
                forward(order(k)).wait_send()


    def sent(i, carry):
        heads_to(order(i // (nb - 1)), lax.rem(mb + 1 + lax.rem(i, nb - 1), nb)).wait_send()
        return carry

    lax.fori_loop(0, nz * (nb - 1), sent, 0)
    for j in range(1, nb):
        back_to(lax.rem(mb + j, nb)).wait_send()
    for n in range(parts):
        for k in range(1, nz):
            sum_to(n, order(k)).wait_send()


def fused(nb, nz, tokens, mod_shift, mod_scale, mod_gate, w_query, w_key, w_value, w_out, score_gain):
    rows = tokens.shape[0]
    cols = w_query.shape[1]
    tile = 512
    parts = D // tile
    bf16, f32 = jnp.bfloat16, jnp.float32
    vmem = pl.BlockSpec(memory_space=pltpu.VMEM)
    hbm = pl.BlockSpec(memory_space=pltpu.HBM)
    dma = pltpu.SemaphoreType.DMA
    return pl.pallas_call(
        functools.partial(kernel, nb, nz),
        out_shape=jax.ShapeDtypeStruct((rows, D), bf16),
        in_specs=[hbm] * 9,
        out_specs=vmem,
        scratch_shapes=[
            pltpu.VMEM((rows, D), bf16),
            pltpu.VMEM((1, D), f32),
            pltpu.VMEM((1, D), f32),
            pltpu.VMEM((1, D), f32),
            pltpu.VMEM((1, HEADS), f32),
            pltpu.VMEM((nz, rows, D), bf16),
            pltpu.VMEM((D, cols), bf16),
            pltpu.VMEM((D, cols), bf16),
            pltpu.VMEM((D, cols), bf16),
            pltpu.VMEM((cols, D), bf16),
            pltpu.VMEM((nz, nb, 2, rows, 128), bf16),
            pltpu.VMEM((2, nb * nz * rows, 128), bf16),
            pltpu.VMEM((nb, nz * rows // 2, 128), bf16),
            pltpu.VMEM((nb, nz * rows // 2, 128), bf16),
            pltpu.VMEM((parts, nz, rows, tile), f32),
            pltpu.VMEM((parts, nz, rows, tile), bf16),
            pltpu.VMEM((parts, nz, rows, tile), bf16),
            dma((9,)),
            dma((nz,)),
            dma((nz,)),
            dma((nz,)),
            dma((nz, nb)),
            dma((nz, nb)),
            dma((nb,)),
            dma((nb,)),
            dma((parts, nz)),
            dma((parts, nz)),
        ],
        compiler_params=pltpu.CompilerParams(
            collective_id=0, has_side_effects=True, vmem_limit_bytes=56 * 1024 * 1024
        ),
    )(
        tokens, mod_shift[None], mod_scale[None], mod_gate[None], score_gain[None],
        w_query, w_key, w_value, w_out,
    )


def modulate(tokens, mod_shift, mod_scale):
    values = tokens.astype(jnp.float32)
    center = values - jnp.mean(values, axis=-1, keepdims=True)
    spread = jnp.mean(center * center, axis=-1, keepdims=True)
    normed = center * lax.rsqrt(spread + 1e-06)
    return (normed * (1.0 + mod_scale) + mod_shift).astype(jnp.bfloat16)


def head_norm(projected, width):
    count = projected.shape[0]
    split = projected.reshape(count, -1, width)
    power = jnp.mean(split * split, axis=-1, keepdims=True)
    return (split * lax.rsqrt(power + 1e-06)).reshape(count, -1).astype(jnp.bfloat16)


def body(tokens, mod_shift, mod_scale, mod_gate, w_query, w_key, w_value, w_out, score_gain):
    width = D // HEADS
    local_cols = w_query.shape[1]
    local_heads = local_cols // width
    modded = modulate(tokens, mod_shift, mod_scale)
    piece = lax.all_gather(modded, "uly", axis=0, tiled=True)
    joined = jnp.concatenate(
        [
            jnp.dot(piece, w_query, preferred_element_type=jnp.float32),
            jnp.dot(piece, w_key, preferred_element_type=jnp.float32),
            jnp.dot(piece, w_value, preferred_element_type=jnp.float32),
        ],
        axis=1,
    )
    queries = head_norm(joined[:, :local_cols], width)
    keys = head_norm(joined[:, local_cols : 2 * local_cols], width)
    values = joined[:, 2 * local_cols :].astype(jnp.bfloat16)
    gains = lax.dynamic_slice_in_dim(score_gain, lax.axis_index("uly") * local_heads, local_heads)
    factors = gains / math.sqrt(width)
    rows = queries.shape[0]
    query_heads = queries.reshape(rows, local_heads, width)
    initial = (
        jnp.full((local_heads, rows), -jnp.inf, jnp.float32),
        jnp.zeros((local_heads, rows), jnp.float32),
        jnp.zeros((local_heads, rows, width), jnp.float32),
    )
    key_piece = lax.all_gather(keys, "blk", axis=0, tiled=True)
    value_piece = lax.all_gather(values, "blk", axis=0, tiled=True)
    count = key_piece.shape[0]
    groups = count // rows
    limit = max(rows, 1024)
    depth = max(
        [step for step in range(1, groups + 1) if groups % step == 0 and step * rows <= limit]
    )
    stride = depth * rows
    key_blocks = key_piece.reshape(count // stride, stride, local_heads, width)
    value_blocks = value_piece.reshape(count // stride, stride, local_heads, width)

    def one_block(carry, blocks):
        run_max, run_total, run_acc = carry
        key_block, value_block = blocks
        scores = jnp.einsum(
            "rhd,khd->hrk", query_heads, key_block, preferred_element_type=jnp.float32
        )
        scores = scores * factors[:, None, None]
        new_max = jnp.maximum(run_max, jnp.max(scores, axis=-1))
        expo = jnp.exp(scores - new_max[..., None])
        rescale = jnp.exp(run_max - new_max)
        new_total = run_total * rescale + jnp.sum(expo, axis=-1)
        summed = jnp.einsum(
            "hrk,khd->hrd",
            expo.astype(jnp.bfloat16),
            value_block,
            preferred_element_type=jnp.float32,
        )
        new_acc = run_acc * rescale[..., None] + summed
        return ((new_max, new_total, new_acc), None)

    result, unused = lax.scan(one_block, initial, (key_blocks, value_blocks))
    run_max, run_total, run_acc = result
    attended = (run_acc / run_total[..., None]).astype(jnp.bfloat16)
    attended = attended.transpose(1, 0, 2).reshape(rows, local_cols)
    returned = lax.all_to_all(attended, "uly", split_axis=0, concat_axis=1, tiled=True)
    projected = jnp.dot(
        returned,
        lax.all_gather(w_out, "uly", axis=0, tiled=True),
        preferred_element_type=jnp.float32,
    )
    return (tokens.astype(jnp.float32) + mod_gate * projected).astype(jnp.bfloat16)


def solution(mesh):
    in_specs = (
        P(("blk", "uly"), None),
        P(),
        P(),
        P(),
        P(None, "uly"),
        P(None, "uly"),
        P(None, "uly"),
        P("uly", None),
        P(),
    )
    out_specs = P(("blk", "uly"), None)
    nb, nz = mesh.shape["blk"], mesh.shape["uly"]
    run = body
    if HEADS == nb * nz:
        run = functools.partial(fused, nb, nz)
    return jax.shard_map(run, mesh=mesh, in_specs=in_specs, out_specs=out_specs, check_vma=False)
```

```python
import functools
import math

import jax
import jax.numpy as jnp
from jax import lax
from jax.experimental import pallas as pl
from jax.experimental.pallas import tpu as pltpu
from jax.sharding import PartitionSpec as P

D = 2048
HEADS = 32
LOG2E = math.log2(math.e)
MESH = pl.DeviceIdType.MESH


def kernel(
    nb, nz, tok_h, shift_h, scale_h, gate_h, gain_h, wq, wk, wv, wo, out,
    tok, shift, scale, gate, gain, mod, wq_v, wk_v, wv_v, wo_v, snd, rcv, asnd, arcv, own, rsnd, rrcv, rel,
    wsem, gs, gr, fs, hs, hr, bs, br, rs, rr, ls, lr,
):
    width = D // HEADS
    rows = tok.shape[0]
    block = nz * rows
    half = block // 2
    tile = rrcv.shape[-1]
    parts = D // tile
    mb, mz = lax.axis_index("blk"), lax.axis_index("uly")

    pairs = (
        (tok_h, tok), (shift_h, shift), (scale_h, scale), (wq, wq_v), (wk, wk_v), (wv, wv_v),
        (wo, wo_v), (gate_h, gate), (gain_h, gain),
    )
    loads = [
        pltpu.make_async_copy(src, dst, wsem.at[i])
        for i, (src, dst) in enumerate(pairs)
    ]
    for load in loads:
        load.start()

    barrier = pltpu.get_barrier_semaphore()
    for j in range(1, nz):
        pl.semaphore_signal(barrier, inc=1, device_id={"uly": lax.rem(mz + j, nz)}, device_id_type=MESH)
    for j in range(1, nb):
        pl.semaphore_signal(barrier, inc=1, device_id={"blk": lax.rem(mb + j, nb)}, device_id_type=MESH)

    def order(k):
        if nz != 4:
            return lax.rem(mz + k, nz)
        high = mz // 2
        near = mz + 1 - 2 * lax.rem(mz, 2)
        return jnp.where(k == 0, mz, jnp.where(k == 1, near, jnp.where(k == 2, 2 - high, 3 - 3 * high)))

    for load in loads[:3]:
        load.wait()
    relayed = nz == 4
    direct = (2, 1) if relayed else tuple(range(nz - 1, 0, -1))
    middle = (mz + 1) // 2 == 1

    values = tok[...].astype(jnp.float32)
    center = values - jnp.mean(values, axis=-1, keepdims=True)
    spread = jnp.mean(center * center, axis=-1, keepdims=True)
    normed = center * lax.rsqrt(spread + 1e-06)
    mod[mz] = (normed * (1.0 + scale[...]) + shift[...]).astype(jnp.bfloat16)

    pl.semaphore_wait(barrier, nz - 1 + nb - 1)

    def gather(z):
        return pltpu.make_async_remote_copy(
            src_ref=mod.at[mz], dst_ref=mod.at[mz], send_sem=gs.at[z], recv_sem=gr.at[mz],
            device_id={"uly": z}, device_id_type=MESH)

    def gathered(z):
        return pltpu.make_async_remote_copy(
            src_ref=mod.at[z], dst_ref=mod.at[z], send_sem=gs.at[z], recv_sem=gr.at[z],
            device_id={"uly": z}, device_id_type=MESH)

    def forward(z):
        return pltpu.make_async_remote_copy(
            src_ref=mod.at[z], dst_ref=mod.at[z], send_sem=fs.at[z], recv_sem=gr.at[z],
            device_id={"uly": order(1)}, device_id_type=MESH)

    for k in direct:
        gather(order(k)).start()
    for load in loads[3:6]:
        load.wait()

    def spot(b, z):
        return pl.ds(pl.multiple_of((b * nz + z) * rows, rows), rows)

    def heads_to(z, b):
        return pltpu.make_async_remote_copy(
            src_ref=snd.at[z, b], dst_ref=rcv.at[:, spot(mb, z), :], send_sem=hs.at[z, b],
            recv_sem=hr.at[z, mb], device_id={"blk": b}, device_id_type=MESH)

    def heads_from(z, b):
        return pltpu.make_async_remote_copy(
            src_ref=snd.at[z, b], dst_ref=rcv.at[:, spot(b, z), :], send_sem=hs.at[z, b],
            recv_sem=hr.at[z, b], device_id={"blk": b}, device_id_type=MESH)

    def piece(k, carry):
        z = order(k)

        @pl.when(k > 0)
        def _():
            gathered(z).wait_recv()

        if relayed:

            @pl.when((k > 1) & middle)
            def _():
                forward(z).start()

        x = mod[z]
        query = jnp.dot(x, wq_v[...], preferred_element_type=jnp.float32)
        key = jnp.dot(x, wk_v[...], preferred_element_type=jnp.float32)
        value = jnp.dot(x, wv_v[...], preferred_element_type=jnp.float32)

        def unit(part):
            power = jnp.mean(part * part, axis=-1, keepdims=True)
            return part * lax.rsqrt(power + 1e-06)

        for h in range(nb):
            cols = slice(h * width, (h + 1) * width)
            snd[z, h, 0] = jnp.concatenate([unit(key[:, cols]), value[:, cols]], axis=1).astype(jnp.bfloat16)
            line = unit(query[:, cols])
            snd[z, h, 1] = jnp.concatenate([line, jnp.zeros_like(line)], axis=1).astype(jnp.bfloat16)
        rcv[:, spot(mb, z), :] = snd[z, mb]

        def send(j, carry):
            heads_to(z, lax.rem(mb + j, nb)).start()
            return carry

        lax.fori_loop(1, nb, send, 0)
        return carry

    lax.fori_loop(0, nz, piece, 0)

    def arrive(i, carry):
        heads_from(order(i // (nb - 1)), lax.rem(mb + 1 + lax.rem(i, nb - 1), nb)).wait_recv()
        return carry

    lax.fori_loop(0, nz * (nb - 1), arrive, 0)

    loads[8].wait()
    chosen = lax.broadcasted_iota(jnp.int32, gain.shape, 1) == mz * nb + mb
    factor = jnp.sum(jnp.where(chosen, gain[...], 0.0), axis=-1, keepdims=True) * (LOG2E / math.sqrt(width))

    def back_to(b):
        return pltpu.make_async_remote_copy(
            src_ref=asnd.at[b], dst_ref=arcv.at[mb], send_sem=bs.at[b], recv_sem=br.at[mb],
            device_id={"blk": b}, device_id_type=MESH)

    def back_from(b):
        return pltpu.make_async_remote_copy(
            src_ref=asnd.at[b], dst_ref=arcv.at[b], send_sem=bs.at[b], recv_sem=br.at[b],
            device_id={"blk": b}, device_id_type=MESH)

    def attend(k, carry):
        b = lax.rem(mb + k, nb)
        q = rcv[1, pl.ds(pl.multiple_of(b * block, block), block), :]
        kv = rcv[0]
        scores = lax.dot_general(q, kv, (((1,), (1,)), ((), ())), preferred_element_type=jnp.float32)
        top = jnp.max(scores, axis=-1, keepdims=True)
        expo = jnp.exp2((scores - top) * factor)
        total = jnp.sum(expo, axis=-1, keepdims=True)
        summed = jnp.dot(expo.astype(jnp.bfloat16), kv, preferred_element_type=jnp.float32) / total
        packed = jnp.concatenate([summed[:half, width:], summed[half:, width:]], axis=1)
        asnd[b] = packed.astype(jnp.bfloat16)

        @pl.when(k < nb)
        def _():
            back_to(b).start()

        return carry

    lax.fori_loop(1, nb + 1, attend, 0)
    arcv[mb] = asnd[mb]
    loads[6].wait()
    loads[7].wait()
    for j in range(1, nb):
        back_from(lax.rem(mb + j, nb)).wait_recv()

    pieces = [arcv[h] for h in range(nb)]
    attended = jnp.concatenate(
        [
            jnp.concatenate([part[:, :width] for part in pieces], axis=1),
            jnp.concatenate([part[:, width:] for part in pieces], axis=1),
        ],
        axis=0,
    )

    def sum_to(n, z):
        return pltpu.make_async_remote_copy(
            src_ref=rsnd.at[n, z], dst_ref=rrcv.at[n, mz], send_sem=rs.at[n, z], recv_sem=rr.at[n, mz],
            device_id={"uly": z}, device_id_type=MESH)

    def sum_from(n, z):
        return pltpu.make_async_remote_copy(
            src_ref=rsnd.at[n, z], dst_ref=rrcv.at[n, z], send_sem=rs.at[n, z], recv_sem=rr.at[n, z],
            device_id={"uly": z}, device_id_type=MESH)

    def relay(n, z):
        return pltpu.make_async_remote_copy(
            src_ref=rsnd.at[n, z], dst_ref=rel.at[n, z], send_sem=ls.at[n, z], recv_sem=lr.at[n, z],
            device_id={"uly": order(1)}, device_id_type=MESH)

    for n in range(parts):
        part = jnp.dot(attended, wo_v[:, n * tile : (n + 1) * tile], preferred_element_type=jnp.float32)
        for z in range(nz):
            own[n, z] = part[z * rows : (z + 1) * rows]
            rsnd[n, z] = part[z * rows : (z + 1) * rows].astype(jnp.bfloat16)
        if relayed:

            @pl.when(jnp.logical_not(middle))
            def _():
                for k in (3, 2):
                    relay(n, order(k)).start()
        else:
            for k in range(nz - 1, 0, -1):
                sum_to(n, order(k)).start()
    if relayed:
        for n in range(parts):
            sum_to(n, order(1)).start()

        @pl.when(middle)
        def _():
            for n in range(parts):
                for k in (3, 2):
                    z = order(k)
                    relay(n, z).wait_recv()
                    rsnd[n, z] = (own[n, z] + rel[n, z].astype(jnp.float32)).astype(jnp.bfloat16)
                    sum_to(n, z).start()
    for n in range(parts):
        total = own[n, mz]
        for k in (1, 2) if relayed else range(1, nz):
            z = order(k)
            sum_from(n, z).wait_recv()
            total = total + rrcv[n, z].astype(jnp.float32)
        cols = slice(n * tile, (n + 1) * tile)
        out[:, cols] = (tok[:, cols].astype(jnp.float32) + gate[:, cols] * total).astype(jnp.bfloat16)

    for k in direct:
        gather(order(k)).wait_send()
    if relayed:

        @pl.when(middle)
        def _():
            for k in (2, 3):
                forward(order(k)).wait_send()


    def sent(i, carry):
        heads_to(order(i // (nb - 1)), lax.rem(mb + 1 + lax.rem(i, nb - 1), nb)).wait_send()
        return carry

    lax.fori_loop(0, nz * (nb - 1), sent, 0)
    for j in range(1, nb):
        back_to(lax.rem(mb + j, nb)).wait_send()
    for n in range(parts):
        for k in (1,) if relayed else range(1, nz):
            sum_to(n, order(k)).wait_send()
    if relayed:

        @pl.when(middle)
        def _():
            for n in range(parts):
                for k in (3, 2):
                    sum_to(n, order(k)).wait_send()

        @pl.when(jnp.logical_not(middle))
        def _():
            for n in range(parts):
                for k in (3, 2):
                    relay(n, order(k)).wait_send()


def fused(nb, nz, tokens, mod_shift, mod_scale, mod_gate, w_query, w_key, w_value, w_out, score_gain):
    rows = tokens.shape[0]
    cols = w_query.shape[1]
    tile = 512
    parts = D // tile
    bf16, f32 = jnp.bfloat16, jnp.float32
    vmem = pl.BlockSpec(memory_space=pltpu.VMEM)
    hbm = pl.BlockSpec(memory_space=pltpu.HBM)
    dma = pltpu.SemaphoreType.DMA
    return pl.pallas_call(
        functools.partial(kernel, nb, nz),
        out_shape=jax.ShapeDtypeStruct((rows, D), bf16),
        in_specs=[hbm] * 9,
        out_specs=vmem,
        scratch_shapes=[
            pltpu.VMEM((rows, D), bf16),
            pltpu.VMEM((1, D), f32),
            pltpu.VMEM((1, D), f32),
            pltpu.VMEM((1, D), f32),
            pltpu.VMEM((1, HEADS), f32),
            pltpu.VMEM((nz, rows, D), bf16),
            pltpu.VMEM((D, cols), bf16),
            pltpu.VMEM((D, cols), bf16),
            pltpu.VMEM((D, cols), bf16),
            pltpu.VMEM((cols, D), bf16),
            pltpu.VMEM((nz, nb, 2, rows, 128), bf16),
            pltpu.VMEM((2, nb * nz * rows, 128), bf16),
            pltpu.VMEM((nb, nz * rows // 2, 128), bf16),
            pltpu.VMEM((nb, nz * rows // 2, 128), bf16),
            pltpu.VMEM((parts, nz, rows, tile), f32),
            pltpu.VMEM((parts, nz, rows, tile), bf16),
            pltpu.VMEM((parts, nz, rows, tile), bf16),
            pltpu.VMEM((parts, nz, rows, tile), bf16),
            dma((9,)),
            dma((nz,)),
            dma((nz,)),
            dma((nz,)),
            dma((nz, nb)),
            dma((nz, nb)),
            dma((nb,)),
            dma((nb,)),
            dma((parts, nz)),
            dma((parts, nz)),
            dma((parts, nz)),
            dma((parts, nz)),
        ],
        compiler_params=pltpu.CompilerParams(
            collective_id=0, has_side_effects=True, vmem_limit_bytes=56 * 1024 * 1024
        ),
    )(
        tokens, mod_shift[None], mod_scale[None], mod_gate[None], score_gain[None],
        w_query, w_key, w_value, w_out,
    )


def modulate(tokens, mod_shift, mod_scale):
    values = tokens.astype(jnp.float32)
    center = values - jnp.mean(values, axis=-1, keepdims=True)
    spread = jnp.mean(center * center, axis=-1, keepdims=True)
    normed = center * lax.rsqrt(spread + 1e-06)
    return (normed * (1.0 + mod_scale) + mod_shift).astype(jnp.bfloat16)


def head_norm(projected, width):
    count = projected.shape[0]
    split = projected.reshape(count, -1, width)
    power = jnp.mean(split * split, axis=-1, keepdims=True)
    return (split * lax.rsqrt(power + 1e-06)).reshape(count, -1).astype(jnp.bfloat16)


def body(tokens, mod_shift, mod_scale, mod_gate, w_query, w_key, w_value, w_out, score_gain):
    width = D // HEADS
    local_cols = w_query.shape[1]
    local_heads = local_cols // width
    modded = modulate(tokens, mod_shift, mod_scale)
    piece = lax.all_gather(modded, "uly", axis=0, tiled=True)
    joined = jnp.concatenate(
        [
            jnp.dot(piece, w_query, preferred_element_type=jnp.float32),
            jnp.dot(piece, w_key, preferred_element_type=jnp.float32),
            jnp.dot(piece, w_value, preferred_element_type=jnp.float32),
        ],
        axis=1,
    )
    queries = head_norm(joined[:, :local_cols], width)
    keys = head_norm(joined[:, local_cols : 2 * local_cols], width)
    values = joined[:, 2 * local_cols :].astype(jnp.bfloat16)
    gains = lax.dynamic_slice_in_dim(score_gain, lax.axis_index("uly") * local_heads, local_heads)
    factors = gains / math.sqrt(width)
    rows = queries.shape[0]
    query_heads = queries.reshape(rows, local_heads, width)
    initial = (
        jnp.full((local_heads, rows), -jnp.inf, jnp.float32),
        jnp.zeros((local_heads, rows), jnp.float32),
        jnp.zeros((local_heads, rows, width), jnp.float32),
    )
    key_piece = lax.all_gather(keys, "blk", axis=0, tiled=True)
    value_piece = lax.all_gather(values, "blk", axis=0, tiled=True)
    count = key_piece.shape[0]
    groups = count // rows
    limit = max(rows, 1024)
    depth = max(
        [step for step in range(1, groups + 1) if groups % step == 0 and step * rows <= limit]
    )
    stride = depth * rows
    key_blocks = key_piece.reshape(count // stride, stride, local_heads, width)
    value_blocks = value_piece.reshape(count // stride, stride, local_heads, width)

    def one_block(carry, blocks):
        run_max, run_total, run_acc = carry
        key_block, value_block = blocks
        scores = jnp.einsum(
            "rhd,khd->hrk", query_heads, key_block, preferred_element_type=jnp.float32
        )
        scores = scores * factors[:, None, None]
        new_max = jnp.maximum(run_max, jnp.max(scores, axis=-1))
        expo = jnp.exp(scores - new_max[..., None])
        rescale = jnp.exp(run_max - new_max)
        new_total = run_total * rescale + jnp.sum(expo, axis=-1)
        summed = jnp.einsum(
            "hrk,khd->hrd",
            expo.astype(jnp.bfloat16),
            value_block,
            preferred_element_type=jnp.float32,
        )
        new_acc = run_acc * rescale[..., None] + summed
        return ((new_max, new_total, new_acc), None)

    result, unused = lax.scan(one_block, initial, (key_blocks, value_blocks))
    run_max, run_total, run_acc = result
    attended = (run_acc / run_total[..., None]).astype(jnp.bfloat16)
    attended = attended.transpose(1, 0, 2).reshape(rows, local_cols)
    returned = lax.all_to_all(attended, "uly", split_axis=0, concat_axis=1, tiled=True)
    projected = jnp.dot(
        returned,
        lax.all_gather(w_out, "uly", axis=0, tiled=True),
        preferred_element_type=jnp.float32,
    )
    return (tokens.astype(jnp.float32) + mod_gate * projected).astype(jnp.bfloat16)


def solution(mesh):
    in_specs = (
        P(("blk", "uly"), None),
        P(),
        P(),
        P(),
        P(None, "uly"),
        P(None, "uly"),
        P(None, "uly"),
        P("uly", None),
        P(),
    )
    out_specs = P(("blk", "uly"), None)
    nb, nz = mesh.shape["blk"], mesh.shape["uly"]
    run = body
    if HEADS == nb * nz:
        run = functools.partial(fused, nb, nz)
    return jax.shard_map(run, mesh=mesh, in_specs=in_specs, out_specs=out_specs, check_vma=False)
```
